32 devices in a mesh: tm: 2 (over y), gy: 4 (over z), gz: 4 (over x, core).
Axes of the slice: x: 2, y: 2, z: 4, core: 2. Of those that a mesh axis runs over, the one named last changes fastest.
Arguments:
- inverse_mass: float32 [32, 64, 128], P('gy', 'gz'), may hold values from 0.5 to 2
- actuator_of_cell: int32 [32, 64, 128], P('gy', 'gz'), may hold values from 0 to 31
- plan_ids: int32 [2, 32], P('tm'), may hold values from 0 to 15
- profiles: float32 [16, 9], replicated, may hold values from -4 to 4
- directions: float32 [3, 32], replicated, may hold values from -4 to 4
Outputs:
- predicted_state: float32 [2, 6, 32, 64, 128], P('tm', None, 'gy', 'gz')
The draws below stay inside these ranges and needn't reach their ends.
All inputs are finite; a program needn't handle non-finite values.
Results may differ from the reference program's by a relative error of at most 0.00021.
Values sent between devices are 32-bit elements; how exact they have to be, the bound alone decides.
A program may use at most 64 MiB of HBM per device.

```python
import math
import jax
import jax.numpy as jnp
import numpy as np

NX = 128
STEPS = 8
TERMS = 8
NACT = 32
NPROF = 16
WINDOWS = 2
NY = 32
NZ = 64


def with_ends(entries, key, smallest, top_value):
    extent = entries.shape
    spot = [jax.random.randint(jax.random.fold_in(key, axis), (), 0, extent[axis]) for axis in range(len(extent))]
    entries = entries.at[tuple(spot)].set(smallest)
    longest = extent.index(max(extent))
    spot[longest] = (spot[longest] + 1) % extent[longest]
    return entries.at[tuple(spot)].set(top_value)


def shard_levels(stream_key, dims, cuts, low, largest):
    def one(dim, shards_of):
        steps = jax.random.uniform(jax.random.fold_in(jax.random.fold_in(stream_key, 6), dim), (shards_of,), jnp.float32, low / len(cuts), largest / len(cuts))
        return jnp.repeat(jnp.exp(steps), dims[dim] // shards_of).reshape((-1,) + (1,) * (len(dims) - dim - 1))

    level = one(*cuts[0])
    for cut in cuts[1:]:
        level = level * one(*cut)
    return level


def centred(rng, extent, spread, limit, dtype=jnp.bfloat16):
    return jnp.clip(spread * jax.random.normal(rng, extent, jnp.float32), -limit, limit).astype(dtype)


def setup_inputs(seed: int = 0) -> dict:
    key_of = jax.random.split(jax.random.key(seed), 6)
    inverse_mass = jnp.clip(jnp.exp(math.log(2.0) - 1.3862944 * jax.random.uniform(key_of[0], (NY, NZ, NX), jnp.float32) ** shard_levels(key_of[0], (NY, NZ, NX), ((0, 4), (1, 4)), -0.2, 0.2)), 0.5, 2.0)
    actuator_of_cell = with_ends(jax.random.randint(key_of[1], (NY, NZ, NX), 0, NACT), jax.random.fold_in(key_of[1], 1), 0, NACT - 1).astype(jnp.int32)
    plan_ids = with_ends(jax.random.randint(key_of[2], (WINDOWS, NACT), 0, NPROF), jax.random.fold_in(key_of[2], 1), 0, NPROF - 1).astype(jnp.int32)
    profiles = centred(key_of[3], (NPROF, STEPS + 1), 1.0, 4.0, jnp.float32)
    directions = centred(key_of[4], (3, NACT), 1.0, 4.0, jnp.float32)
    return dict(inverse_mass=inverse_mass, actuator_of_cell=actuator_of_cell, plan_ids=plan_ids, profiles=profiles, directions=directions)


lame_ratio = 2.5
mass_top = 2.0
step_squared = 1.0

def cheb_tables():
    spectrum_top = mass_top * 12.0 * (1.0 + lame_ratio)
    time_step = math.sqrt(step_squared / spectrum_top)
    horizon = STEPS * time_step
    angles = np.pi * (np.arange(TERMS) + 0.5) / TERMS
    node_x = 0.5 * spectrum_top * (1.0 + np.cos(angles))
    node_root = np.sqrt(node_x)
    values_c = np.cos(horizon * node_root)
    values_s = np.sin(horizon * node_root) / node_root
    values_g = node_root * np.sin(horizon * node_root)

    def project_values(values):
        result = np.array([2.0 / TERMS * np.sum(values * np.cos(k * angles)) for k in range(TERMS)])
        result[0] = 0.5 * result[0]
        return [float(entry) for entry in result]
    return (spectrum_top, time_step, project_values(values_c), project_values(values_s), project_values(values_g))

def stiffness(padded, inverse_mass):
    size_y = padded.shape[-3] - 2
    size_z = padded.shape[-2] - 2
    size_x = padded.shape[-1] - 2
    centre = padded[..., 1:size_y + 1, 1:size_z + 1, 1:size_x + 1]
    beside = padded[..., 2:, 1:size_z + 1, 1:size_x + 1] + padded[..., :size_y, 1:size_z + 1, 1:size_x + 1]
    beside = beside + padded[..., 1:size_y + 1, 2:, 1:size_x + 1] + padded[..., 1:size_y + 1, :size_z, 1:size_x + 1]
    beside = beside + padded[..., 1:size_y + 1, 1:size_z + 1, 2:] + padded[..., 1:size_y + 1, 1:size_z + 1, :size_x]
    laplace_term = 6.0 * centre - beside
    lower = padded[..., :size_y + 1, :size_z + 1, :size_x + 1]
    divergence = padded[..., 0, 1:, :size_z + 1, :size_x + 1] - lower[..., 0, :, :, :]
    divergence = divergence + (padded[..., 1, :size_y + 1, 1:, :size_x + 1] - lower[..., 1, :, :, :])
    divergence = divergence + (padded[..., 2, :size_y + 1, :size_z + 1, 1:] - lower[..., 2, :, :, :])
    inner = divergence[..., 1:, 1:, 1:]
    gradient = jnp.stack([divergence[..., :size_y, 1:, 1:] - inner, divergence[..., 1:, :size_z, 1:] - inner, divergence[..., 1:, 1:, :size_x] - inner], axis=-4)
    return inverse_mass * (laplace_term + lame_ratio * gradient)

def pad_full(field):
    return jnp.pad(field, [(0, 0)] * (field.ndim - 3) + [(1, 1)] * 3)

def leapfrog(force, amplitude, apply_op):
    spectrum_top, time_step, coef_c, coef_s, coef_g = cheb_tables()
    half_step = 0.5 * time_step
    displace = jnp.zeros_like(force)
    velocity = jnp.zeros_like(force)
    stiff_term = jnp.zeros_like(force)
    for n in range(STEPS):
        half_velocity = velocity + half_step * (force * amplitude[n] - stiff_term)
        displace = displace + time_step * half_velocity
        stiff_term = apply_op(displace)
        velocity = half_velocity + half_step * (force * amplitude[n + 1] - stiff_term)
    return jnp.concatenate([displace, velocity], axis=0)

def propagate(state, apply_op):
    spectrum_top, time_step, coef_c, coef_s, coef_g = cheb_tables()
    scale = 2.0 / spectrum_top
    second_table = jnp.asarray([[coef_g[k], coef_s[k]] for k in range(TERMS)], jnp.float32).reshape(TERMS, 2, 1, 1, 1, 1)
    previous = state.reshape((2, 3) + state.shape[1:])
    first = coef_c[0] * previous
    second = second_table[0] * previous
    current = scale * apply_op(previous) - previous
    for k in range(1, TERMS):
        first = first + coef_c[k] * current
        second = second + second_table[k] * current
        if k < TERMS - 1:
            shifted = scale * apply_op(current) - current
            previous, current = (current, 2.0 * shifted - previous)
    new_displace = first[0] + second[1]
    new_velocity = first[1] - second[0]
    return jnp.concatenate([new_displace, new_velocity], axis=0)

def reference(inverse_mass, actuator_of_cell, plan_ids, profiles, directions):

    def apply_op(field):
        return stiffness(pad_full(field), inverse_mass)
    force = inverse_mass[None] * directions[:, actuator_of_cell]
    end_states = []
    moved_once = []
    moved_twice = []
    for w in range(WINDOWS):
        chosen = profiles[plan_ids[w]]
        amplitude = jnp.moveaxis(chosen[actuator_of_cell], -1, 0)
        end_state = leapfrog(force, amplitude, apply_op)
        moved = propagate(end_state, apply_op)
        end_states.append(end_state)
        moved_once.append(moved)
        moved_twice.append(propagate(moved, apply_op))
    outputs = []
    for w in range(WINDOWS):
        total = end_states[w]
        total = total + (moved_once[w - 1] if w >= 1 else jnp.zeros_like(total))
        total = total + (moved_twice[w - 2] if w >= 2 else jnp.zeros_like(total))
        outputs.append(total)
    return jnp.stack(outputs)
```

```python
import functools
import math

import jax
import jax.numpy as jnp
import numpy as np
from jax import lax
from jax.experimental import pallas as pl
from jax.experimental.pallas import tpu as pltpu
from jax.sharding import PartitionSpec as P

STEPS = 8
TERMS = 8
LANES = 128
MESH = pl.DeviceIdType.MESH

lame_ratio = 2.5
mass_top = 2.0
step_squared = 1.0


def cheb_tables():
    spectrum_top = mass_top * 12.0 * (1.0 + lame_ratio)
    time_step = math.sqrt(step_squared / spectrum_top)
    horizon = STEPS * time_step
    angles = np.pi * (np.arange(TERMS) + 0.5) / TERMS
    node_x = 0.5 * spectrum_top * (1.0 + np.cos(angles))
    node_root = np.sqrt(node_x)
    values_c = np.cos(horizon * node_root)
    values_s = np.sin(horizon * node_root) / node_root
    values_g = node_root * np.sin(horizon * node_root)

    def project_values(values):
        result = np.array([2.0 / TERMS * np.sum(values * np.cos(k * angles)) for k in range(TERMS)])
        result[0] = 0.5 * result[0]
        return [float(entry) for entry in result]

    return (
        spectrum_top,
        time_step,
        project_values(values_c),
        project_values(values_s),
        project_values(values_g),
    )


def down(field, first):
    rows = lax.broadcasted_iota(jnp.int32, field.shape, 0)
    return jnp.where(rows == 0, first, pltpu.roll(field, 1, 0))


def up(field, last):
    size = field.shape[0]
    rows = lax.broadcasted_iota(jnp.int32, field.shape, 0)
    return jnp.where(rows == size - 1, last, pltpu.roll(field, size - 1, 0))


def x_down(field, first):
    lanes = lax.broadcasted_iota(jnp.int32, field.shape, 1)
    return jnp.where(lanes == 0, first, pltpu.roll(field, 1, 1))


def x_up(field):
    size = field.shape[1]
    lanes = lax.broadcasted_iota(jnp.int32, field.shape, 1)
    return jnp.where(lanes == size - 1, 0.0, pltpu.roll(field, size - 1, 1))


def kernel(
    sizes,
    mass_ref,
    act_ref,
    table_ref,
    coef_ref,
    out_ref,
    tabs,
    tab_rows,
    amp,
    force,
    disp,
    vel,
    cheb,
    y_in,
    z_in,
    d_in,
    send_sem,
    recv_sem,
    tab_send,
    tab_recv,
):
    count_t, count_y, count_z, windows, count_act = sizes
    size_y, size_z, size_x = mass_ref.shape
    spectrum_top, time_step, _, _, _ = cheb_tables()
    scale = 2.0 / spectrum_top
    at_t, at_y, at_z = (lax.axis_index(name) for name in ("tm", "gy", "gz"))
    has_low_y, has_high_y = at_y > 0, at_y < count_y - 1
    has_low_z, has_high_z = at_z > 0, at_z < count_z - 1
    beside = [
        (has_low_y, {"gy": at_y - 1}),
        (has_high_y, {"gy": at_y + 1}),
        (has_low_z, {"gz": at_z - 1}),
        (has_high_z, {"gz": at_z + 1}),
        (jnp.logical_and(has_low_y, has_high_z), {"gy": at_y - 1, "gz": at_z + 1}),
        (jnp.logical_and(has_high_y, has_low_z), {"gy": at_y + 1, "gz": at_z - 1}),
    ]
    later = [(at_t + s < count_t, {"tm": at_t + s}) for s in range(1, windows)]
    earlier = [(at_t - s >= 0, {"tm": at_t - s}) for s in range(1, windows)]

    y_in[...] = jnp.zeros_like(y_in)
    z_in[...] = jnp.zeros_like(z_in)
    d_in[...] = jnp.zeros_like(d_in)
    tabs[...] = jnp.zeros_like(tabs)

    barrier = pltpu.get_barrier_semaphore()
    everyone = beside + later + earlier
    for exists, device in everyone:

        @pl.when(exists)
        def _(device=device):
            pl.semaphore_signal(barrier, inc=1, device_id=device, device_id_type=MESH)

    peers = 0
    for exists, _ in everyone:
        peers = peers + jnp.where(exists, 1, 0)
    pl.semaphore_wait(barrier, peers)

    def table_copy(s, device):
        return pltpu.make_async_remote_copy(
            src_ref=table_ref,
            dst_ref=tabs.at[s - 1],
            send_sem=tab_send.at[s - 1],
            recv_sem=tab_recv.at[s - 1],
            device_id=device,
            device_id_type=MESH,
        )

    for s in range(1, windows):
        exists, device = later[s - 1]

        @pl.when(exists)
        def _(s=s, device=device):
            table_copy(s, device).start()

    def spread(s, table):
        for a in range(count_act):
            tab_rows[s, a] = jnp.broadcast_to(table[:, a : a + 1], table.shape)

    spread(0, table_ref[...])
    for s in range(1, windows):
        exists, device = later[s - 1]
        here, source = earlier[s - 1]

        @pl.when(here)
        def _(s=s, source=source):
            table_copy(s, source).wait_recv()

        spread(s, tabs[s - 1])

        @pl.when(exists)
        def _(s=s, device=device):
            table_copy(s, device).wait_send()

    times = STEPS + 1
    entries = [(s, n) for s in range(windows) for n in range(times)]
    entries += [(0, times + c) for c in range(3)]

    def look_up(y, carry):
        act = act_ref[y]
        mass = mass_ref[y]

        def one(a, values):
            hit = act == a
            return tuple(
                jnp.where(hit, tab_rows[s, a, r : r + 1, :], value)
                for (s, r), value in zip(entries, values)
            )

        zero = jnp.zeros((size_z, size_x), jnp.float32)
        values = lax.fori_loop(0, count_act, one, tuple(zero for _ in entries))
        for (s, r), value in zip(entries, values):
            if r < times:
                amp[s, r, y] = value
        for c in range(3):
            force[c, y] = mass * values[windows * times + c]
        for s in range(windows):
            for c in range(3):
                half = (0.5 * time_step) * (force[c, y] * values[s * times])
                vel[s, c, y] = half
                disp[0, s, c, y] = time_step * half
        return carry

    lax.fori_loop(0, size_y, look_up, 0)

    def copies(field, states, slot):
        top, end = size_y - 1, size_z - 1
        pairs = [
            (field.at[:, :, 0:1], y_in.at[slot, 1, 0:states]),
            (field.at[:, :, top : top + 1], y_in.at[slot, 0, 0:states]),
            (field.at[:, :, :, 0:1], z_in.at[slot, 1, 0:states]),
            (field.at[:, :, :, end : end + 1], z_in.at[slot, 0, 0:states]),
            (field.at[:, 0:1, 0:1, end : end + 1], d_in.at[slot, 1, 0:states]),
            (field.at[:, 1:2, top : top + 1, 0:1], d_in.at[slot, 0, 0:states]),
        ]
        opposite = (1, 0, 3, 2, 5, 4)
        made = []
        for i, ((source, target), (exists, device)) in enumerate(zip(pairs, beside)):
            made.append(
                (
                    exists,
                    pltpu.make_async_remote_copy(
                        src_ref=source,
                        dst_ref=target,
                        send_sem=send_sem.at[slot, i],
                        recv_sem=recv_sem.at[slot, opposite[i]],
                        device_id=device,
                        device_id_type=MESH,
                    ),
                )
            )
        return made

    def start(field, states, slot):
        for exists, copy in copies(field, states, slot):

            @pl.when(exists)
            def _(copy=copy):
                copy.start()

    def finish(field, states, slot):
        made = copies(field, states, slot)
        for i in range(6):
            exists = beside[i][0]

            @pl.when(exists)
            def _(i=i):
                made[(1, 0, 3, 2, 5, 4)[i]][1].wait_recv()

        for exists, copy in made:

            @pl.when(exists)
            def _(copy=copy):
                copy.wait_send()

    def stiffness(field, s, slot, use):
        def get(c, y):
            if y < 0:
                return y_in[slot, 0, s, c, 0]
            if y == size_y:
                return y_in[slot, 1, s, c, 0]
            return field[s, c, y]

        def divergence(y, u_y, u_z, u_x, above_y, last_z):
            value = (above_y - u_y) + (up(u_z, last_z) - u_z)
            return value + (x_up(u_x) - u_x)

        u_low = [get(c, -1) for c in range(3)]
        u = [get(c, 0) for c in range(3)]
        corner = d_in[slot, 0, s, 0, 0]
        p_low = divergence(-1, u_low[0], u_low[1], u_low[2], u[0], corner)
        for y in range(size_y):
            u_high = [get(c, y + 1) for c in range(3)]
            z_low = [z_in[slot, 0, s, c, y] for c in range(3)]
            z_high = [z_in[slot, 1, s, c, y] for c in range(3)]
            if y < size_y - 1:
                z_low_above = z_in[slot, 0, s, 0, y + 1]
            else:
                z_low_above = d_in[slot, 1, s, 0, 0]
            u_ups = up(u[1], z_high[1])
            x_ups = x_up(u[2])
            p = ((u_high[0] - u[0]) + (u_ups - u[1])) + (x_ups - u[2])
            p_edge = (z_low_above - z_low[0]) + (u[1][0:1] - z_low[1])
            p_edge = p_edge + (x_up(z_low[2]) - z_low[2])
            inner = [p_low - p, down(p, p_edge) - p, x_down(p, u[2]) - p]
            mass = mass_ref[y]
            for c in range(3):
                total = u_high[c] + u_low[c]
                z_up = u_ups if c == 1 else up(u[c], z_high[c])
                total = total + (z_up + down(u[c], z_low[c]))
                xs = x_ups if c == 2 else x_up(u[c])
                total = total + (xs + x_down(u[c], 0.0))
                use(c, y, u[c], mass * ((6.0 * u[c] - total) + lame_ratio * inner[c]))
            u_low, u, p_low = u, u_high, p

    def forced(n, carry):
        slot = lax.rem(n, 2)
        other = 1 - slot
        field = disp.at[slot]
        start(field, windows, slot)
        is_last = n == STEPS - 1
        kick = jnp.where(is_last, 0.5 * time_step, time_step).astype(jnp.float32)
        drift = jnp.where(is_last, 0.0, time_step).astype(jnp.float32)
        finish(field, windows, slot)
        for s in range(windows):

            def use(c, y, u, stiff, s=s):
                half = vel[s, c, y] + kick * (force[c, y] * amp[s, n + 1, y] - stiff)
                vel[s, c, y] = half
                disp[other, s, c, y] = u + drift * half

            stiffness(field, s, slot, use)
        return carry

    lax.fori_loop(0, STEPS, forced, 0)
    final = STEPS % 2

    out_ref[0, 0:3] = disp[final, 0]
    out_ref[0, 3:6] = vel[0]
    if windows > 1:
        cheb[0, 0] = disp[final, windows - 1]
        cheb[0, 1] = vel[windows - 1]

    def add_term(k, slot, goal_u, goal_v):
        cc, cs, cg = coef_ref[0, k], coef_ref[1, k], coef_ref[2, k]
        for c in range(3):
            for y in range(size_y):
                t_u, t_v = cheb[slot, 0, c, y], cheb[slot, 1, c, y]
                goal_u[c, y] = goal_u[c, y] + (cc * t_u + cs * t_v)
                goal_v[c, y] = goal_v[c, y] + (cc * t_v - cg * t_u)

    base = STEPS
    for w in range(windows - 1, 0, -1):
        if w == 1:
            goal_u, goal_v = out_ref.at[0, 0:3], out_ref.at[0, 3:6]
        else:
            goal_u, goal_v = disp.at[final, w - 1], vel.at[w - 1]
        cheb[1] = jnp.zeros(cheb.shape[1:], jnp.float32)

        def term(k, carry, base=base, goal_u=goal_u, goal_v=goal_v):
            slot = lax.rem(k, 2)
            other = 1 - slot
            wire = lax.rem(k + base, 2)
            field = cheb.at[slot]
            start(field, 2, wire)
            add_term(k, slot, goal_u, goal_v)
            lead = jnp.where(k == 0, 1.0, 2.0).astype(jnp.float32)
            finish(field, 2, wire)
            for s in range(2):

                def use(c, y, u, stiff, s=s):
                    cheb[other, s, c, y] = lead * (scale * stiff - u) - cheb[other, s, c, y]

                stiffness(field, s, wire, use)
            return carry

        lax.fori_loop(0, TERMS - 1, term, 0)
        add_term(TERMS - 1, (TERMS - 1) % 2, goal_u, goal_v)
        base += TERMS - 1
        if w > 1:
            cheb[0, 0] = disp[final, w - 1]
            cheb[0, 1] = vel[w - 1]


def body(counts, inverse_mass, actuator_of_cell, plan_ids, profiles, directions):
    size_y, size_z, size_x = inverse_mass.shape
    count_act = directions.shape[1]
    count_prof, times = profiles.shape
    windows = min(counts[0], 3)
    wide = -(-count_act // LANES) * LANES
    rows = -(-(times + 3) // 8) * 8
    picked = plan_ids[0][None, None, :] == jnp.arange(count_prof, dtype=jnp.int32)[None, :, None]
    chosen = jnp.sum(jnp.where(picked, profiles.T[:, :, None], 0.0), axis=1)
    table = jnp.concatenate([chosen, directions], axis=0)
    table = jnp.pad(table, ((0, rows - times - 3), (0, wide - count_act)))
    _, _, coef_c, coef_s, coef_g = cheb_tables()
    coefs = jnp.asarray(np.array([coef_c, coef_s, coef_g], np.float32))
    block = (size_y, size_z, size_x)
    most = max(windows, 2)
    f32 = jnp.float32
    vmem = pl.BlockSpec(memory_space=pltpu.VMEM)
    return pl.pallas_call(
        functools.partial(kernel, counts + (windows, count_act)),
        out_shape=jax.ShapeDtypeStruct((1, 6) + block, f32),
        in_specs=[vmem, vmem, vmem, pl.BlockSpec(memory_space=pltpu.SMEM)],
        out_specs=vmem,
        scratch_shapes=[
            pltpu.VMEM((most - 1, rows, wide), f32),
            pltpu.VMEM((windows, count_act, rows, size_x), f32),
            pltpu.VMEM((windows, times) + block, f32),
            pltpu.VMEM((3,) + block, f32),
            pltpu.VMEM((2, windows, 3) + block, f32),
            pltpu.VMEM((windows, 3) + block, f32),
            pltpu.VMEM((2, 2, 3) + block, f32),
            pltpu.VMEM((2, 2, most, 3, 1, size_z, size_x), f32),
            pltpu.VMEM((2, 2, most, 3, size_y, 1, size_x), f32),
            pltpu.VMEM((2, 2, most, 1, 1, 1, size_x), f32),
            pltpu.SemaphoreType.DMA((2, 6)),
            pltpu.SemaphoreType.DMA((2, 6)),
            pltpu.SemaphoreType.DMA((most - 1,)),
            pltpu.SemaphoreType.DMA((most - 1,)),
        ],
        compiler_params=pltpu.CompilerParams(
            collective_id=0, has_side_effects=True, vmem_limit_bytes=32 * 1024 * 1024
        ),
    )(inverse_mass, actuator_of_cell, table, coefs)


def solution(mesh):
    counts = (mesh.shape["tm"], mesh.shape["gy"], mesh.shape["gz"])
    in_specs = (P("gy", "gz", None), P("gy", "gz", None), P("tm", None), P(), P())
    out_specs = P("tm", None, "gy", "gz", None)
    return jax.shard_map(
        functools.partial(body, counts),
        mesh=mesh,
        in_specs=in_specs,
        out_specs=out_specs,
        check_vma=False,
    )
```

```python
import functools
import math

import jax
import jax.numpy as jnp
import numpy as np
from jax import lax
from jax.experimental import pallas as pl
from jax.experimental.pallas import tpu as pltpu
from jax.sharding import PartitionSpec as P

STEPS = 8
TERMS = 8
LANES = 128
MESH = pl.DeviceIdType.MESH

lame_ratio = 2.5
mass_top = 2.0
step_squared = 1.0


def cheb_tables():
    spectrum_top = mass_top * 12.0 * (1.0 + lame_ratio)
    time_step = math.sqrt(step_squared / spectrum_top)
    horizon = STEPS * time_step
    angles = np.pi * (np.arange(TERMS) + 0.5) / TERMS
    node_x = 0.5 * spectrum_top * (1.0 + np.cos(angles))
    node_root = np.sqrt(node_x)
    values_c = np.cos(horizon * node_root)
    values_s = np.sin(horizon * node_root) / node_root
    values_g = node_root * np.sin(horizon * node_root)

    def project_values(values):
        result = np.array([2.0 / TERMS * np.sum(values * np.cos(k * angles)) for k in range(TERMS)])
        result[0] = 0.5 * result[0]
        return [float(entry) for entry in result]

    return (
        spectrum_top,
        time_step,
        project_values(values_c),
        project_values(values_s),
        project_values(values_g),
    )


def down(field, first):
    rows = lax.broadcasted_iota(jnp.int32, field.shape, 0)
    return jnp.where(rows == 0, first, pltpu.roll(field, 1, 0))


def up(field, last):
    size = field.shape[0]
    rows = lax.broadcasted_iota(jnp.int32, field.shape, 0)
    return jnp.where(rows == size - 1, last, pltpu.roll(field, size - 1, 0))


def x_down(field, first):
    lanes = lax.broadcasted_iota(jnp.int32, field.shape, 1)
    return jnp.where(lanes == 0, first, pltpu.roll(field, 1, 1))


def x_up(field):
    size = field.shape[1]
    lanes = lax.broadcasted_iota(jnp.int32, field.shape, 1)
    return jnp.where(lanes == size - 1, 0.0, pltpu.roll(field, size - 1, 1))


def kernel(
    sizes,
    mass_ref,
    act_ref,
    table_ref,
    coef_ref,
    out_ref,
    tabs,
    tab_rows,
    amp,
    force,
    disp,
    vel,
    cheb,
    y_in,
    z_in,
    d_in,
    send_sem,
    recv_sem,
    tab_send,
    tab_recv,
):
    count_t, count_y, count_z, windows, count_act = sizes
    size_y, size_z, size_x = mass_ref.shape
    spectrum_top, time_step, _, _, _ = cheb_tables()
    scale = 2.0 / spectrum_top
    at_t, at_y, at_z = (lax.axis_index(name) for name in ("tm", "gy", "gz"))
    has_low_y, has_high_y = at_y > 0, at_y < count_y - 1
    has_low_z, has_high_z = at_z > 0, at_z < count_z - 1
    beside = [
        (has_low_y, {"gy": at_y - 1}),
        (has_high_y, {"gy": at_y + 1}),
        (has_low_z, {"gz": at_z - 1}),
        (has_high_z, {"gz": at_z + 1}),
        (jnp.logical_and(has_low_y, has_high_z), {"gy": at_y - 1, "gz": at_z + 1}),
        (jnp.logical_and(has_high_y, has_low_z), {"gy": at_y + 1, "gz": at_z - 1}),
    ]
    later = [(at_t + s < count_t, {"tm": at_t + s}) for s in range(1, windows)]
    earlier = [(at_t - s >= 0, {"tm": at_t - s}) for s in range(1, windows)]

    y_in[...] = jnp.zeros_like(y_in)
    z_in[...] = jnp.zeros_like(z_in)
    d_in[...] = jnp.zeros_like(d_in)
    tabs[...] = jnp.zeros_like(tabs)

    barrier = pltpu.get_barrier_semaphore()
    everyone = beside + later + earlier
    for exists, device in everyone:

        @pl.when(exists)
        def _(device=device):
            pl.semaphore_signal(barrier, inc=1, device_id=device, device_id_type=MESH)

    peers = 0
    for exists, _ in everyone:
        peers = peers + jnp.where(exists, 1, 0)
    pl.semaphore_wait(barrier, peers)

    def table_copy(s, device):
        return pltpu.make_async_remote_copy(
            src_ref=table_ref,
            dst_ref=tabs.at[s - 1],
            send_sem=tab_send.at[s - 1],
            recv_sem=tab_recv.at[s - 1],
            device_id=device,
            device_id_type=MESH,
        )

    for s in range(1, windows):
        exists, device = later[s - 1]

        @pl.when(exists)
        def _(s=s, device=device):
            table_copy(s, device).start()

    def spread(s, table):
        for a in range(count_act):
            tab_rows[s, a] = jnp.broadcast_to(table[:, a : a + 1], table.shape)

    spread(0, table_ref[...])
    for s in range(1, windows):
        exists, device = later[s - 1]
        here, source = earlier[s - 1]

        @pl.when(here)
        def _(s=s, source=source):
            table_copy(s, source).wait_recv()

        spread(s, tabs[s - 1])

        @pl.when(exists)
        def _(s=s, device=device):
            table_copy(s, device).wait_send()

    times = STEPS + 1
    entries = [(s, n) for s in range(windows) for n in range(times)]
    entries += [(0, times + c) for c in range(3)]

    def look_up(y, carry):
        act = act_ref[y]
        mass = mass_ref[y]

        def one(a, values):
            hit = act == a
            return tuple(
                jnp.where(hit, tab_rows[s, a, r : r + 1, :], value)
                for (s, r), value in zip(entries, values)
            )

        zero = jnp.zeros((size_z, size_x), jnp.float32)
        values = lax.fori_loop(0, count_act, one, tuple(zero for _ in entries))
        for (s, r), value in zip(entries, values):
            if r < times:
                amp[s, r, y] = value
        for c in range(3):
            force[c, y] = mass * values[windows * times + c]
        for s in range(windows):
            for c in range(3):
                half = (0.5 * time_step) * (force[c, y] * values[s * times])
                vel[s, c, y] = half
                disp[0, s, c, y] = time_step * half
        return carry

    lax.fori_loop(0, size_y, look_up, 0)

    def copies(field, s, slot):
        top, end = size_y - 1, size_z - 1
        pairs = [
            (field.at[:, 0:1], y_in.at[slot, 1, s]),
            (field.at[:, top : top + 1], y_in.at[slot, 0, s]),
            (field.at[:, :,  0:1], z_in.at[slot, 1, s]),
            (field.at[:, :,  end : end + 1], z_in.at[slot, 0, s]),
            (field.at[0:1, 0:1, end : end + 1], d_in.at[slot, 1, s]),
            (field.at[1:2, top : top + 1, 0:1], d_in.at[slot, 0, s]),
        ]
        opposite = (1, 0, 3, 2, 5, 4)
        made = []
        for i, ((source, target), (exists, device)) in enumerate(zip(pairs, beside)):
            made.append(
                (
                    exists,
                    pltpu.make_async_remote_copy(
                        src_ref=source,
                        dst_ref=target,
                        send_sem=send_sem.at[slot, s, i],
                        recv_sem=recv_sem.at[slot, s, opposite[i]],
                        device_id=device,
                        device_id_type=MESH,
                    ),
                )
            )
        return made

    def start(field, s, slot):
        for exists, copy in copies(field, s, slot):

            @pl.when(exists)
            def _(copy=copy):
                copy.start()

    def finish(field, s, slot):
        made = copies(field, s, slot)
        for i in range(6):
            exists = beside[i][0]

            @pl.when(exists)
            def _(i=i):
                made[(1, 0, 3, 2, 5, 4)[i]][1].wait_recv()

        for exists, copy in made:

            @pl.when(exists)
            def _(copy=copy):
                copy.wait_send()

    def stiffness(field, s, slot, use):
        def get(c, y):
            if y < 0:
                return y_in[slot, 0, s, c, 0]
            if y == size_y:
                return y_in[slot, 1, s, c, 0]
            return field[s, c, y]

        def divergence(y, u_y, u_z, u_x, above_y, last_z):
            value = (above_y - u_y) + (up(u_z, last_z) - u_z)
            return value + (x_up(u_x) - u_x)

        u_low = [get(c, -1) for c in range(3)]
        u = [get(c, 0) for c in range(3)]
        corner = d_in[slot, 0, s, 0, 0]
        p_low = divergence(-1, u_low[0], u_low[1], u_low[2], u[0], corner)
        for y in range(size_y):
            u_high = [get(c, y + 1) for c in range(3)]
            z_low = [z_in[slot, 0, s, c, y] for c in range(3)]
            z_high = [z_in[slot, 1, s, c, y] for c in range(3)]
            if y < size_y - 1:
                z_low_above = z_in[slot, 0, s, 0, y + 1]
            else:
                z_low_above = d_in[slot, 1, s, 0, 0]
            u_ups = up(u[1], z_high[1])
            x_ups = x_up(u[2])
            p = ((u_high[0] - u[0]) + (u_ups - u[1])) + (x_ups - u[2])
            p_edge = (z_low_above - z_low[0]) + (u[1][0:1] - z_low[1])
            p_edge = p_edge + (x_up(z_low[2]) - z_low[2])
            inner = [p_low - p, down(p, p_edge) - p, x_down(p, u[2]) - p]
            mass = mass_ref[y]
            for c in range(3):
                total = u_high[c] + u_low[c]
                z_up = u_ups if c == 1 else up(u[c], z_high[c])
                total = total + (z_up + down(u[c], z_low[c]))
                xs = x_ups if c == 2 else x_up(u[c])
                total = total + (xs + x_down(u[c], 0.0))
                use(c, y, u[c], mass * ((6.0 * u[c] - total) + lame_ratio * inner[c]))
            u_low, u, p_low = u, u_high, p

    def forced(n, carry):
        slot = lax.rem(n, 2)
        other = 1 - slot
        field = disp.at[slot]
        is_last = n == STEPS - 1
        kick = jnp.where(is_last, 0.5 * time_step, time_step).astype(jnp.float32)
        drift = jnp.where(is_last, 0.0, time_step).astype(jnp.float32)
        for s in range(windows):

            def use(c, y, u, stiff, s=s):
                half = vel[s, c, y] + kick * (force[c, y] * amp[s, n + 1, y] - stiff)
                vel[s, c, y] = half
                disp[other, s, c, y] = u + drift * half

            finish(disp.at[slot, s], s, slot)
            stiffness(field, s, slot, use)

            @pl.when(n < STEPS - 1)
            def _(s=s):
                start(disp.at[other, s], s, other)

        return carry

    for s in range(windows):
        start(disp.at[0, s], s, 0)
    lax.fori_loop(0, STEPS, forced, 0)
    final = STEPS % 2

    out_ref[0, 0:3] = disp[final, 0]
    out_ref[0, 3:6] = vel[0]
    if windows > 1:
        cheb[0, 0] = disp[final, windows - 1]
        cheb[0, 1] = vel[windows - 1]

    def add_term(k, slot, goal_u, goal_v):
        cc, cs, cg = coef_ref[0, k], coef_ref[1, k], coef_ref[2, k]
        for c in range(3):
            for y in range(size_y):
                t_u, t_v = cheb[slot, 0, c, y], cheb[slot, 1, c, y]
                goal_u[c, y] = goal_u[c, y] + (cc * t_u + cs * t_v)
                goal_v[c, y] = goal_v[c, y] + (cc * t_v - cg * t_u)

    base = STEPS
    for w in range(windows - 1, 0, -1):
        if w == 1:
            goal_u, goal_v = out_ref.at[0, 0:3], out_ref.at[0, 3:6]
        else:
            goal_u, goal_v = disp.at[final, w - 1], vel.at[w - 1]
        cheb[1] = jnp.zeros(cheb.shape[1:], jnp.float32)

        def term(k, carry, base=base, goal_u=goal_u, goal_v=goal_v):
            slot = lax.rem(k, 2)
            other = 1 - slot
            wire = lax.rem(k + base, 2)
            field = cheb.at[slot]
            add_term(k, slot, goal_u, goal_v)
            lead = jnp.where(k == 0, 1.0, 2.0).astype(jnp.float32)
            for s in range(2):

                def use(c, y, u, stiff, s=s):
                    cheb[other, s, c, y] = lead * (scale * stiff - u) - cheb[other, s, c, y]

                finish(cheb.at[slot, s], s, wire)
                stiffness(field, s, wire, use)

                @pl.when(k < TERMS - 2)
                def _(s=s):
                    start(cheb.at[other, s], s, 1 - wire)

            return carry

        for s in range(2):
            start(cheb.at[0, s], s, base % 2)
        lax.fori_loop(0, TERMS - 1, term, 0)
        add_term(TERMS - 1, (TERMS - 1) % 2, goal_u, goal_v)
        base += TERMS - 1
        if w > 1:
            cheb[0, 0] = disp[final, w - 1]
            cheb[0, 1] = vel[w - 1]


def body(counts, inverse_mass, actuator_of_cell, plan_ids, profiles, directions):
    size_y, size_z, size_x = inverse_mass.shape
    count_act = directions.shape[1]
    count_prof, times = profiles.shape
    windows = min(counts[0], 3)
    wide = -(-count_act // LANES) * LANES
    rows = -(-(times + 3) // 8) * 8
    picked = plan_ids[0][None, None, :] == jnp.arange(count_prof, dtype=jnp.int32)[None, :, None]
    chosen = jnp.sum(jnp.where(picked, profiles.T[:, :, None], 0.0), axis=1)
    table = jnp.concatenate([chosen, directions], axis=0)
    table = jnp.pad(table, ((0, rows - times - 3), (0, wide - count_act)))
    _, _, coef_c, coef_s, coef_g = cheb_tables()
    coefs = jnp.asarray(np.array([coef_c, coef_s, coef_g], np.float32))
    block = (size_y, size_z, size_x)
    most = max(windows, 2)
    f32 = jnp.float32
    vmem = pl.BlockSpec(memory_space=pltpu.VMEM)
    return pl.pallas_call(
        functools.partial(kernel, counts + (windows, count_act)),
        out_shape=jax.ShapeDtypeStruct((1, 6) + block, f32),
        in_specs=[vmem, vmem, vmem, pl.BlockSpec(memory_space=pltpu.SMEM)],
        out_specs=vmem,
        scratch_shapes=[
            pltpu.VMEM((most - 1, rows, wide), f32),
            pltpu.VMEM((windows, count_act, rows, size_x), f32),
            pltpu.VMEM((windows, times) + block, f32),
            pltpu.VMEM((3,) + block, f32),
            pltpu.VMEM((2, windows, 3) + block, f32),
            pltpu.VMEM((windows, 3) + block, f32),
            pltpu.VMEM((2, 2, 3) + block, f32),
            pltpu.VMEM((2, 2, most, 3, 1, size_z, size_x), f32),
            pltpu.VMEM((2, 2, most, 3, size_y, 1, size_x), f32),
            pltpu.VMEM((2, 2, most, 1, 1, 1, size_x), f32),
            pltpu.SemaphoreType.DMA((2, most, 6)),
            pltpu.SemaphoreType.DMA((2, most, 6)),
            pltpu.SemaphoreType.DMA((most - 1,)),
            pltpu.SemaphoreType.DMA((most - 1,)),
        ],
        compiler_params=pltpu.CompilerParams(
            collective_id=0, has_side_effects=True, vmem_limit_bytes=32 * 1024 * 1024
        ),
    )(inverse_mass, actuator_of_cell, table, coefs)


def solution(mesh):
    counts = (mesh.shape["tm"], mesh.shape["gy"], mesh.shape["gz"])
    in_specs = (P("gy", "gz", None), P("gy", "gz", None), P("tm", None), P(), P())
    out_specs = P("tm", None, "gy", "gz", None)
    return jax.shard_map(
        functools.partial(body, counts),
        mesh=mesh,
        in_specs=in_specs,
        out_specs=out_specs,
        check_vma=False,
    )
```

```python
import functools
import math

import jax
import jax.numpy as jnp
import numpy as np
from jax import lax
from jax.experimental import pallas as pl
from jax.experimental.pallas import tpu as pltpu
from jax.sharding import PartitionSpec as P

STEPS = 8
TERMS = 8
LANES = 128
MESH = pl.DeviceIdType.MESH

lame_ratio = 2.5
mass_top = 2.0
step_squared = 1.0


def cheb_tables():
    spectrum_top = mass_top * 12.0 * (1.0 + lame_ratio)
    time_step = math.sqrt(step_squared / spectrum_top)
    horizon = STEPS * time_step
    angles = np.pi * (np.arange(TERMS) + 0.5) / TERMS
    node_x = 0.5 * spectrum_top * (1.0 + np.cos(angles))
    node_root = np.sqrt(node_x)
    values_c = np.cos(horizon * node_root)
    values_s = np.sin(horizon * node_root) / node_root
    values_g = node_root * np.sin(horizon * node_root)

    def project_values(values):
        result = np.array([2.0 / TERMS * np.sum(values * np.cos(k * angles)) for k in range(TERMS)])
        result[0] = 0.5 * result[0]
        return [float(entry) for entry in result]

    return (
        spectrum_top,
        time_step,
        project_values(values_c),
        project_values(values_s),
        project_values(values_g),
    )


def down(field, first):
    rows = lax.broadcasted_iota(jnp.int32, field.shape, 0)
    return jnp.where(rows == 0, first, pltpu.roll(field, 1, 0))


def up(field, last):
    size = field.shape[0]
    rows = lax.broadcasted_iota(jnp.int32, field.shape, 0)
    return jnp.where(rows == size - 1, last, pltpu.roll(field, size - 1, 0))


def x_down(field, first):
    lanes = lax.broadcasted_iota(jnp.int32, field.shape, 1)
    return jnp.where(lanes == 0, first, pltpu.roll(field, 1, 1))


def x_up(field):
    size = field.shape[1]
    lanes = lax.broadcasted_iota(jnp.int32, field.shape, 1)
    return jnp.where(lanes == size - 1, 0.0, pltpu.roll(field, size - 1, 1))


def kernel(
    sizes,
    mass_ref,
    act_ref,
    table_ref,
    coef_ref,
    out_ref,
    tabs,
    tab_rows,
    amp,
    force,
    disp,
    vel,
    cheb,
    y_in,
    z_in,
    d_in,
    send_sem,
    recv_sem,
    tab_send,
    tab_recv,
):
    count_t, count_y, count_z, windows, count_act = sizes
    size_y, size_z, size_x = mass_ref.shape
    spectrum_top, time_step, _, _, _ = cheb_tables()
    scale = 2.0 / spectrum_top
    at_t, at_y, at_z = (lax.axis_index(name) for name in ("tm", "gy", "gz"))
    has_low_y, has_high_y = at_y > 0, at_y < count_y - 1
    has_low_z, has_high_z = at_z > 0, at_z < count_z - 1
    beside = [
        (has_low_y, {"gy": at_y - 1}),
        (has_high_y, {"gy": at_y + 1}),
        (has_low_z, {"gz": at_z - 1}),
        (has_high_z, {"gz": at_z + 1}),
        (jnp.logical_and(has_low_y, has_high_z), {"gy": at_y - 1, "gz": at_z + 1}),
        (jnp.logical_and(has_high_y, has_low_z), {"gy": at_y + 1, "gz": at_z - 1}),
    ]
    later = [(at_t + s < count_t, {"tm": at_t + s}) for s in range(1, windows)]
    earlier = [(at_t - s >= 0, {"tm": at_t - s}) for s in range(1, windows)]

    y_in[...] = jnp.zeros_like(y_in)
    z_in[...] = jnp.zeros_like(z_in)
    d_in[...] = jnp.zeros_like(d_in)
    tabs[...] = jnp.zeros_like(tabs)

    barrier = pltpu.get_barrier_semaphore()
    everyone = beside + later + earlier
    for exists, device in everyone:

        @pl.when(exists)
        def _(device=device):
            pl.semaphore_signal(barrier, inc=1, device_id=device, device_id_type=MESH)

    def spread(s, table):
        for a in range(count_act):
            tab_rows[s, a] = jnp.broadcast_to(table[:, a : a + 1], table.shape)

    spread(0, table_ref[...])
    peers = 0
    for exists, _ in everyone:
        peers = peers + jnp.where(exists, 1, 0)
    pl.semaphore_wait(barrier, peers)

    def table_copy(s, device):
        return pltpu.make_async_remote_copy(
            src_ref=table_ref,
            dst_ref=tabs.at[s - 1],
            send_sem=tab_send.at[s - 1],
            recv_sem=tab_recv.at[s - 1],
            device_id=device,
            device_id_type=MESH,
        )

    for s in range(1, windows):
        exists, device = later[s - 1]

        @pl.when(exists)
        def _(s=s, device=device):
            table_copy(s, device).start()

    for s in range(1, windows):
        exists, device = later[s - 1]
        here, source = earlier[s - 1]

        @pl.when(here)
        def _(s=s, source=source):
            table_copy(s, source).wait_recv()

        spread(s, tabs[s - 1])

        @pl.when(exists)
        def _(s=s, device=device):
            table_copy(s, device).wait_send()

    times = STEPS + 1
    entries = [(s, n) for s in range(windows) for n in range(times)]
    entries += [(0, times + c) for c in range(3)]

    def look_up(y, carry):
        act = act_ref[y]
        mass = mass_ref[y]

        def one(a, values):
            hit = act == a
            return tuple(
                jnp.where(hit, tab_rows[s, a, r : r + 1, :], value)
                for (s, r), value in zip(entries, values)
            )

        zero = jnp.zeros((size_z, size_x), jnp.float32)
        values = lax.fori_loop(0, count_act, one, tuple(zero for _ in entries))
        for (s, r), value in zip(entries, values):
            if r < times:
                amp[s, r, y] = value
        for c in range(3):
            force[c, y] = mass * values[windows * times + c]
        for s in range(windows):
            for c in range(3):
                half = (0.5 * time_step) * (force[c, y] * values[s * times])
                vel[s, c, y] = half
                disp[0, s, c, y] = time_step * half
        return carry

    lax.fori_loop(0, size_y, look_up, 0)

    def copies(field, s, slot):
        top, end = size_y - 1, size_z - 1
        pairs = [
            (field.at[:, 0:1], y_in.at[slot, 1, s]),
            (field.at[:, top : top + 1], y_in.at[slot, 0, s]),
            (field.at[:, :,  0:1], z_in.at[slot, 1, s]),
            (field.at[:, :,  end : end + 1], z_in.at[slot, 0, s]),
            (field.at[0:1, 0:1, end : end + 1], d_in.at[slot, 1, s]),
            (field.at[1:2, top : top + 1, 0:1], d_in.at[slot, 0, s]),
        ]
        opposite = (1, 0, 3, 2, 5, 4)
        made = []
        for i, ((source, target), (exists, device)) in enumerate(zip(pairs, beside)):
            made.append(
                (
                    exists,
                    pltpu.make_async_remote_copy(
                        src_ref=source,
                        dst_ref=target,
                        send_sem=send_sem.at[slot, s, i],
                        recv_sem=recv_sem.at[slot, s, opposite[i]],
                        device_id=device,
                        device_id_type=MESH,
                    ),
                )
            )
        return made

    def start(field, s, slot, first=0, stop=6):
        for exists, copy in copies(field, s, slot)[first:stop]:

            @pl.when(exists)
            def _(copy=copy):
                copy.start()

    def finish(field, s, slot):
        made = copies(field, s, slot)
        for i in range(6):
            exists = beside[i][0]

            @pl.when(exists)
            def _(i=i):
                made[(1, 0, 3, 2, 5, 4)[i]][1].wait_recv()

        for exists, copy in made:

            @pl.when(exists)
            def _(copy=copy):
                copy.wait_send()

    def stiffness(field, s, slot, use):
        def get(c, y):
            if y < 0:
                return y_in[slot, 0, s, c, 0]
            if y == size_y:
                return y_in[slot, 1, s, c, 0]
            return field[s, c, y]

        def divergence(y, u_y, u_z, u_x, above_y, last_z):
            value = (above_y - u_y) + (up(u_z, last_z) - u_z)
            return value + (x_up(u_x) - u_x)

        u_low = [get(c, -1) for c in range(3)]
        u = [get(c, 0) for c in range(3)]
        corner = d_in[slot, 0, s, 0, 0]
        p_low = divergence(-1, u_low[0], u_low[1], u_low[2], u[0], corner)
        for y in range(size_y):
            u_high = [get(c, y + 1) for c in range(3)]
            z_low = [z_in[slot, 0, s, c, y] for c in range(3)]
            z_high = [z_in[slot, 1, s, c, y] for c in range(3)]
            if y < size_y - 1:
                z_low_above = z_in[slot, 0, s, 0, y + 1]
            else:
                z_low_above = d_in[slot, 1, s, 0, 0]
            u_ups = up(u[1], z_high[1])
            x_ups = x_up(u[2])
            p = ((u_high[0] - u[0]) + (u_ups - u[1])) + (x_ups - u[2])
            p_edge = (z_low_above - z_low[0]) + (u[1][0:1] - z_low[1])
            p_edge = p_edge + (x_up(z_low[2]) - z_low[2])
            inner = [p_low - p, down(p, p_edge) - p, x_down(p, u[2]) - p]
            mass = mass_ref[y]
            for c in range(3):
                total = u_high[c] + u_low[c]
                z_up = u_ups if c == 1 else up(u[c], z_high[c])
                total = total + (z_up + down(u[c], z_low[c]))
                xs = x_ups if c == 2 else x_up(u[c])
                total = total + (xs + x_down(u[c], 0.0))
                use(c, y, u[c], mass * ((6.0 * u[c] - total) + lame_ratio * inner[c]))
            u_low, u, p_low = u, u_high, p

    def forced(n, carry):
        slot = lax.rem(n, 2)
        other = 1 - slot
        field = disp.at[slot]
        is_last = n == STEPS - 1
        kick = jnp.where(is_last, 0.5 * time_step, time_step).astype(jnp.float32)
        drift = jnp.where(is_last, 0.0, time_step).astype(jnp.float32)
        for s in range(windows):

            def use(c, y, u, stiff, s=s):
                half = vel[s, c, y] + kick * (force[c, y] * amp[s, n + 1, y] - stiff)
                vel[s, c, y] = half
                disp[other, s, c, y] = u + drift * half
                if c == 2 and y == 0:

                    @pl.when(n < STEPS - 1)
                    def _():
                        start(disp.at[other, s], s, other, 0, 1)

            finish(disp.at[slot, s], s, slot)
            stiffness(field, s, slot, use)

            @pl.when(n < STEPS - 1)
            def _(s=s):
                start(disp.at[other, s], s, other, 1)

        return carry

    for s in range(windows):
        start(disp.at[0, s], s, 0)
    lax.fori_loop(0, STEPS, forced, 0)
    final = STEPS % 2

    out_ref[0, 0:3] = disp[final, 0]
    out_ref[0, 3:6] = vel[0]
    if windows > 1:
        cheb[0, 0] = disp[final, windows - 1]
        cheb[0, 1] = vel[windows - 1]

    def add_term(k, slot, goal_u, goal_v):
        cc, cs, cg = coef_ref[0, k], coef_ref[1, k], coef_ref[2, k]
        for c in range(3):
            for y in range(size_y):
                t_u, t_v = cheb[slot, 0, c, y], cheb[slot, 1, c, y]
                goal_u[c, y] = goal_u[c, y] + (cc * t_u + cs * t_v)
                goal_v[c, y] = goal_v[c, y] + (cc * t_v - cg * t_u)

    base = STEPS
    for w in range(windows - 1, 0, -1):
        if w == 1:
            goal_u, goal_v = out_ref.at[0, 0:3], out_ref.at[0, 3:6]
        else:
            goal_u, goal_v = disp.at[final, w - 1], vel.at[w - 1]
        cheb[1] = jnp.zeros(cheb.shape[1:], jnp.float32)

        def term(k, carry, base=base, goal_u=goal_u, goal_v=goal_v):
            slot = lax.rem(k, 2)
            other = 1 - slot
            wire = lax.rem(k + base, 2)
            field = cheb.at[slot]
            add_term(k, slot, goal_u, goal_v)
            lead = jnp.where(k == 0, 1.0, 2.0).astype(jnp.float32)
            for s in range(2):

                def use(c, y, u, stiff, s=s):
                    cheb[other, s, c, y] = lead * (scale * stiff - u) - cheb[other, s, c, y]
                    if c == 2 and y == 0:

                        @pl.when(k < TERMS - 2)
                        def _():
                            start(cheb.at[other, s], s, 1 - wire, 0, 1)

                finish(cheb.at[slot, s], s, wire)
                stiffness(field, s, wire, use)

                @pl.when(k < TERMS - 2)
                def _(s=s):
                    start(cheb.at[other, s], s, 1 - wire, 1)

            return carry

        for s in range(2):
            start(cheb.at[0, s], s, base % 2)
        lax.fori_loop(0, TERMS - 1, term, 0)
        add_term(TERMS - 1, (TERMS - 1) % 2, goal_u, goal_v)
        base += TERMS - 1
        if w > 1:
            cheb[0, 0] = disp[final, w - 1]
            cheb[0, 1] = vel[w - 1]


def body(counts, inverse_mass, actuator_of_cell, plan_ids, profiles, directions):
    size_y, size_z, size_x = inverse_mass.shape
    count_act = directions.shape[1]
    count_prof, times = profiles.shape
    windows = min(counts[0], 3)
    wide = -(-count_act // LANES) * LANES
    rows = -(-(times + 3) // 8) * 8
    picked = plan_ids[0][None, None, :] == jnp.arange(count_prof, dtype=jnp.int32)[None, :, None]
    chosen = jnp.sum(jnp.where(picked, profiles.T[:, :, None], 0.0), axis=1)
    table = jnp.concatenate([chosen, directions], axis=0)
    table = jnp.pad(table, ((0, rows - times - 3), (0, wide - count_act)))
    _, _, coef_c, coef_s, coef_g = cheb_tables()
    coefs = jnp.asarray(np.array([coef_c, coef_s, coef_g], np.float32))
    block = (size_y, size_z, size_x)
    most = max(windows, 2)
    f32 = jnp.float32
    vmem = pl.BlockSpec(memory_space=pltpu.VMEM)
    return pl.pallas_call(
        functools.partial(kernel, counts + (windows, count_act)),
        out_shape=jax.ShapeDtypeStruct((1, 6) + block, f32),
        in_specs=[vmem, vmem, vmem, pl.BlockSpec(memory_space=pltpu.SMEM)],
        out_specs=vmem,
        scratch_shapes=[
            pltpu.VMEM((most - 1, rows, wide), f32),
            pltpu.VMEM((windows, count_act, rows, size_x), f32),
            pltpu.VMEM((windows, times) + block, f32),
            pltpu.VMEM((3,) + block, f32),
            pltpu.VMEM((2, windows, 3) + block, f32),
            pltpu.VMEM((windows, 3) + block, f32),
            pltpu.VMEM((2, 2, 3) + block, f32),
            pltpu.VMEM((2, 2, most, 3, 1, size_z, size_x), f32),
            pltpu.VMEM((2, 2, most, 3, size_y, 1, size_x), f32),
            pltpu.VMEM((2, 2, most, 1, 1, 1, size_x), f32),
            pltpu.SemaphoreType.DMA((2, most, 6)),
            pltpu.SemaphoreType.DMA((2, most, 6)),
            pltpu.SemaphoreType.DMA((most - 1,)),
            pltpu.SemaphoreType.DMA((most - 1,)),
        ],
        compiler_params=pltpu.CompilerParams(
            collective_id=0, has_side_effects=True, vmem_limit_bytes=32 * 1024 * 1024
        ),
    )(inverse_mass, actuator_of_cell, table, coefs)


def solution(mesh):
    counts = (mesh.shape["tm"], mesh.shape["gy"], mesh.shape["gz"])
    in_specs = (P("gy", "gz", None), P("gy", "gz", None), P("tm", None), P(), P())
    out_specs = P("tm", None, "gy", "gz", None)
    return jax.shard_map(
        functools.partial(body, counts),
        mesh=mesh,
        in_specs=in_specs,
        out_specs=out_specs,
        check_vma=False,
    )
```

```python
import functools
import math

import jax
import jax.numpy as jnp
import numpy as np
from jax import lax
from jax.experimental import pallas as pl
from jax.experimental.pallas import tpu as pltpu
from jax.sharding import PartitionSpec as P

STEPS = 8
TERMS = 8
LANES = 128
UNROLL = 4
MESH = pl.DeviceIdType.MESH

lame_ratio = 2.5
mass_top = 2.0
step_squared = 1.0


def cheb_tables():
    spectrum_top = mass_top * 12.0 * (1.0 + lame_ratio)
    time_step = math.sqrt(step_squared / spectrum_top)
    horizon = STEPS * time_step
    angles = np.pi * (np.arange(TERMS) + 0.5) / TERMS
    node_x = 0.5 * spectrum_top * (1.0 + np.cos(angles))
    node_root = np.sqrt(node_x)
    values_c = np.cos(horizon * node_root)
    values_s = np.sin(horizon * node_root) / node_root
    values_g = node_root * np.sin(horizon * node_root)

    def project_values(values):
        result = np.array([2.0 / TERMS * np.sum(values * np.cos(k * angles)) for k in range(TERMS)])
        result[0] = 0.5 * result[0]
        return [float(entry) for entry in result]

    return (
        spectrum_top,
        time_step,
        project_values(values_c),
        project_values(values_s),
        project_values(values_g),
    )


def down(field, first):
    rows = lax.broadcasted_iota(jnp.int32, field.shape, 0)
    return jnp.where(rows == 0, first, pltpu.roll(field, 1, 0))


def up(field, last):
    size = field.shape[0]
    rows = lax.broadcasted_iota(jnp.int32, field.shape, 0)
    return jnp.where(rows == size - 1, last, pltpu.roll(field, size - 1, 0))


def x_down(field, first):
    lanes = lax.broadcasted_iota(jnp.int32, field.shape, 1)
    return jnp.where(lanes == 0, first, pltpu.roll(field, 1, 1))


def x_up(field):
    size = field.shape[1]
    lanes = lax.broadcasted_iota(jnp.int32, field.shape, 1)
    return jnp.where(lanes == size - 1, 0.0, pltpu.roll(field, size - 1, 1))


def kernel(
    sizes,
    mass_ref,
    act_ref,
    table_ref,
    coef_ref,
    out_ref,
    tabs,
    tab_rows,
    amp,
    force,
    disp,
    vel,
    cheb,
    y_in,
    z_in,
    d_in,
    send_sem,
    recv_sem,
    tab_send,
    tab_recv,
):
    count_t, count_y, count_z, windows, count_act = sizes
    size_y, size_z, size_x = mass_ref.shape
    spectrum_top, time_step, _, _, _ = cheb_tables()
    scale = 2.0 / spectrum_top
    at_t, at_y, at_z = (lax.axis_index(name) for name in ("tm", "gy", "gz"))
    has_low_y, has_high_y = at_y > 0, at_y < count_y - 1
    has_low_z, has_high_z = at_z > 0, at_z < count_z - 1
    beside = [
        (has_low_y, {"gy": at_y - 1}),
        (has_high_y, {"gy": at_y + 1}),
        (has_low_z, {"gz": at_z - 1}),
        (has_high_z, {"gz": at_z + 1}),
        (jnp.logical_and(has_low_y, has_high_z), {"gy": at_y - 1, "gz": at_z + 1}),
        (jnp.logical_and(has_high_y, has_low_z), {"gy": at_y + 1, "gz": at_z - 1}),
    ]
    later = [(at_t + s < count_t, {"tm": at_t + s}) for s in range(1, windows)]
    earlier = [(at_t - s >= 0, {"tm": at_t - s}) for s in range(1, windows)]

    y_in[...] = jnp.zeros_like(y_in)
    z_in[...] = jnp.zeros_like(z_in)
    d_in[...] = jnp.zeros_like(d_in)
    tabs[...] = jnp.zeros_like(tabs)

    barrier = pltpu.get_barrier_semaphore()
    everyone = beside + later + earlier
    for exists, device in everyone:

        @pl.when(exists)
        def _(device=device):
            pl.semaphore_signal(barrier, inc=1, device_id=device, device_id_type=MESH)

    peers = 0
    for exists, _ in everyone:
        peers = peers + jnp.where(exists, 1, 0)
    pl.semaphore_wait(barrier, peers)

    def table_copy(s, device):
        return pltpu.make_async_remote_copy(
            src_ref=table_ref,
            dst_ref=tabs.at[s - 1],
            send_sem=tab_send.at[s - 1],
            recv_sem=tab_recv.at[s - 1],
            device_id=device,
            device_id_type=MESH,
        )

    for s in range(1, windows):
        exists, device = later[s - 1]

        @pl.when(exists)
        def _(s=s, device=device):
            table_copy(s, device).start()

    def spread(s, table):
        for a in range(count_act):
            tab_rows[s, a] = jnp.broadcast_to(table[:, a : a + 1], table.shape)

    spread(0, table_ref[...])
    for s in range(1, windows):
        exists, device = later[s - 1]
        here, source = earlier[s - 1]

        @pl.when(here)
        def _(s=s, source=source):
            table_copy(s, source).wait_recv()

        spread(s, tabs[s - 1])

        @pl.when(exists)
        def _(s=s, device=device):
            table_copy(s, device).wait_send()

    times = STEPS + 1
    early = [(s, 0) for s in range(windows)] + [(0, times + c) for c in range(3)]
    late = [(s, n) for s in range(windows) for n in range(1, times)]

    def look_up(y, entries):
        act = act_ref[y]

        def one(a, values):
            hit = act == a
            return tuple(
                jnp.where(hit, tab_rows[s, a, r : r + 1, :], value)
                for (s, r), value in zip(entries, values)
            )

        zero = jnp.zeros((size_z, size_x), jnp.float32)
        start_values = tuple(zero for _ in entries)
        return lax.fori_loop(0, count_act, one, start_values, unroll=UNROLL)

    def first_step(y, carry):
        values = look_up(y, early)
        for c in range(3):
            force[c, y] = mass_ref[y] * values[windows + c]
        for s in range(windows):
            for c in range(3):
                half = (0.5 * time_step) * (force[c, y] * values[s])
                vel[s, c, y] = half
                disp[0, s, c, y] = time_step * half
        return carry

    lax.fori_loop(0, size_y, first_step, 0)

    def later_amplitudes(y, carry):
        for (s, n), value in zip(late, look_up(y, late)):
            amp[s, n, y] = value
        return carry

    def copies(field, s, slot):
        top, end = size_y - 1, size_z - 1
        pairs = [
            (field.at[:, 0:1], y_in.at[slot, 1, s]),
            (field.at[:, top : top + 1], y_in.at[slot, 0, s]),
            (field.at[:, :,  0:1], z_in.at[slot, 1, s]),
            (field.at[:, :,  end : end + 1], z_in.at[slot, 0, s]),
            (field.at[0:1, 0:1, end : end + 1], d_in.at[slot, 1, s]),
            (field.at[1:2, top : top + 1, 0:1], d_in.at[slot, 0, s]),
        ]
        opposite = (1, 0, 3, 2, 5, 4)
        made = []
        for i, ((source, target), (exists, device)) in enumerate(zip(pairs, beside)):
            made.append(
                (
                    exists,
                    pltpu.make_async_remote_copy(
                        src_ref=source,
                        dst_ref=target,
                        send_sem=send_sem.at[slot, s, i],
                        recv_sem=recv_sem.at[slot, s, opposite[i]],
                        device_id=device,
                        device_id_type=MESH,
                    ),
                )
            )
        return made

    def start(field, s, slot):
        for exists, copy in copies(field, s, slot):

            @pl.when(exists)
            def _(copy=copy):
                copy.start()

    def finish(field, s, slot):
        made = copies(field, s, slot)
        for i in range(6):
            exists = beside[i][0]

            @pl.when(exists)
            def _(i=i):
                made[(1, 0, 3, 2, 5, 4)[i]][1].wait_recv()

        for exists, copy in made:

            @pl.when(exists)
            def _(copy=copy):
                copy.wait_send()

    def stiffness(field, s, slot, use):
        def get(c, y):
            if y < 0:
                return y_in[slot, 0, s, c, 0]
            if y == size_y:
                return y_in[slot, 1, s, c, 0]
            return field[s, c, y]

        def divergence(y, u_y, u_z, u_x, above_y, last_z):
            value = (above_y - u_y) + (up(u_z, last_z) - u_z)
            return value + (x_up(u_x) - u_x)

        u_low = [get(c, -1) for c in range(3)]
        u = [get(c, 0) for c in range(3)]
        corner = d_in[slot, 0, s, 0, 0]
        p_low = divergence(-1, u_low[0], u_low[1], u_low[2], u[0], corner)
        for y in range(size_y):
            u_high = [get(c, y + 1) for c in range(3)]
            z_low = [z_in[slot, 0, s, c, y] for c in range(3)]
            z_high = [z_in[slot, 1, s, c, y] for c in range(3)]
            if y < size_y - 1:
                z_low_above = z_in[slot, 0, s, 0, y + 1]
            else:
                z_low_above = d_in[slot, 1, s, 0, 0]
            u_ups = up(u[1], z_high[1])
            x_ups = x_up(u[2])
            p = ((u_high[0] - u[0]) + (u_ups - u[1])) + (x_ups - u[2])
            p_edge = (z_low_above - z_low[0]) + (u[1][0:1] - z_low[1])
            p_edge = p_edge + (x_up(z_low[2]) - z_low[2])
            inner = [p_low - p, down(p, p_edge) - p, x_down(p, u[2]) - p]
            mass = mass_ref[y]
            for c in range(3):
                total = u_high[c] + u_low[c]
                z_up = u_ups if c == 1 else up(u[c], z_high[c])
                total = total + (z_up + down(u[c], z_low[c]))
                xs = x_ups if c == 2 else x_up(u[c])
                total = total + (xs + x_down(u[c], 0.0))
                use(c, y, u[c], mass * ((6.0 * u[c] - total) + lame_ratio * inner[c]))
            u_low, u, p_low = u, u_high, p

    def forced(n, carry):
        slot = lax.rem(n, 2)
        other = 1 - slot
        field = disp.at[slot]
        is_last = n == STEPS - 1
        kick = jnp.where(is_last, 0.5 * time_step, time_step).astype(jnp.float32)
        drift = jnp.where(is_last, 0.0, time_step).astype(jnp.float32)
        for s in range(windows):

            def use(c, y, u, stiff, s=s):
                half = vel[s, c, y] + kick * (force[c, y] * amp[s, n + 1, y] - stiff)
                vel[s, c, y] = half
                disp[other, s, c, y] = u + drift * half

            finish(disp.at[slot, s], s, slot)
            stiffness(field, s, slot, use)

            @pl.when(n < STEPS - 1)
            def _(s=s):
                start(disp.at[other, s], s, other)

        return carry

    for s in range(windows):
        start(disp.at[0, s], s, 0)
    lax.fori_loop(0, size_y, later_amplitudes, 0)
    lax.fori_loop(0, STEPS, forced, 0)
    final = STEPS % 2

    out_ref[0, 0:3] = disp[final, 0]
    out_ref[0, 3:6] = vel[0]
    if windows > 1:
        cheb[0, 0] = disp[final, windows - 1]
        cheb[0, 1] = vel[windows - 1]

    def add_term(k, slot, goal_u, goal_v):
        cc, cs, cg = coef_ref[0, k], coef_ref[1, k], coef_ref[2, k]
        for c in range(3):
            for y in range(size_y):
                t_u, t_v = cheb[slot, 0, c, y], cheb[slot, 1, c, y]
                goal_u[c, y] = goal_u[c, y] + (cc * t_u + cs * t_v)
                goal_v[c, y] = goal_v[c, y] + (cc * t_v - cg * t_u)

    base = STEPS
    for w in range(windows - 1, 0, -1):
        if w == 1:
            goal_u, goal_v = out_ref.at[0, 0:3], out_ref.at[0, 3:6]
        else:
            goal_u, goal_v = disp.at[final, w - 1], vel.at[w - 1]
        cheb[1] = jnp.zeros(cheb.shape[1:], jnp.float32)

        def term(k, carry, base=base, goal_u=goal_u, goal_v=goal_v):
            slot = lax.rem(k, 2)
            other = 1 - slot
            wire = lax.rem(k + base, 2)
            field = cheb.at[slot]
            add_term(k, slot, goal_u, goal_v)
            lead = jnp.where(k == 0, 1.0, 2.0).astype(jnp.float32)
            for s in range(2):

                def use(c, y, u, stiff, s=s):
                    cheb[other, s, c, y] = lead * (scale * stiff - u) - cheb[other, s, c, y]

                finish(cheb.at[slot, s], s, wire)
                stiffness(field, s, wire, use)

                @pl.when(k < TERMS - 2)
                def _(s=s):
                    start(cheb.at[other, s], s, 1 - wire)

            return carry

        for s in range(2):
            start(cheb.at[0, s], s, base % 2)
        lax.fori_loop(0, TERMS - 1, term, 0)
        add_term(TERMS - 1, (TERMS - 1) % 2, goal_u, goal_v)
        base += TERMS - 1
        if w > 1:
            cheb[0, 0] = disp[final, w - 1]
            cheb[0, 1] = vel[w - 1]


def body(counts, inverse_mass, actuator_of_cell, plan_ids, profiles, directions):
    size_y, size_z, size_x = inverse_mass.shape
    count_act = directions.shape[1]
    count_prof, times = profiles.shape
    windows = min(counts[0], 3)
    wide = -(-count_act // LANES) * LANES
    rows = -(-(times + 3) // 8) * 8
    picked = plan_ids[0][None, None, :] == jnp.arange(count_prof, dtype=jnp.int32)[None, :, None]
    chosen = jnp.sum(jnp.where(picked, profiles.T[:, :, None], 0.0), axis=1)
    table = jnp.concatenate([chosen, directions], axis=0)
    table = jnp.pad(table, ((0, rows - times - 3), (0, wide - count_act)))
    _, _, coef_c, coef_s, coef_g = cheb_tables()
    coefs = jnp.asarray(np.array([coef_c, coef_s, coef_g], np.float32))
    block = (size_y, size_z, size_x)
    most = max(windows, 2)
    f32 = jnp.float32
    vmem = pl.BlockSpec(memory_space=pltpu.VMEM)
    return pl.pallas_call(
        functools.partial(kernel, counts + (windows, count_act)),
        out_shape=jax.ShapeDtypeStruct((1, 6) + block, f32),
        in_specs=[vmem, vmem, vmem, pl.BlockSpec(memory_space=pltpu.SMEM)],
        out_specs=vmem,
        scratch_shapes=[
            pltpu.VMEM((most - 1, rows, wide), f32),
            pltpu.VMEM((windows, count_act, rows, size_x), f32),
            pltpu.VMEM((windows, times) + block, f32),
            pltpu.VMEM((3,) + block, f32),
            pltpu.VMEM((2, windows, 3) + block, f32),
            pltpu.VMEM((windows, 3) + block, f32),
            pltpu.VMEM((2, 2, 3) + block, f32),
            pltpu.VMEM((2, 2, most, 3, 1, size_z, size_x), f32),
            pltpu.VMEM((2, 2, most, 3, size_y, 1, size_x), f32),
            pltpu.VMEM((2, 2, most, 1, 1, 1, size_x), f32),
            pltpu.SemaphoreType.DMA((2, most, 6)),
            pltpu.SemaphoreType.DMA((2, most, 6)),
            pltpu.SemaphoreType.DMA((most - 1,)),
            pltpu.SemaphoreType.DMA((most - 1,)),
        ],
        compiler_params=pltpu.CompilerParams(
            collective_id=0, has_side_effects=True, vmem_limit_bytes=32 * 1024 * 1024
        ),
    )(inverse_mass, actuator_of_cell, table, coefs)


def solution(mesh):
    counts = (mesh.shape["tm"], mesh.shape["gy"], mesh.shape["gz"])
    in_specs = (P("gy", "gz", None), P("gy", "gz", None), P("tm", None), P(), P())
    out_specs = P("tm", None, "gy", "gz", None)
    return jax.shard_map(
        functools.partial(body, counts),
        mesh=mesh,
        in_specs=in_specs,
        out_specs=out_specs,
        check_vma=False,
    )
```
